32 devices in a mesh: ctx: 8 (over z, x), head: 4 (over y, core).
Axes of the slice: x: 2, y: 2, z: 4, core: 2. Of those that a mesh axis runs over, the one named last changes fastest.
Arguments:
- query_rows: bfloat16 [24576, 4096], P('ctx', 'head'), may hold values from -6 to 6
- key_rows: bfloat16 [24576, 4096], P('ctx', 'head'), may hold values from -6 to 6
- value_rows: bfloat16 [24576, 4096], P('ctx', 'head'), may hold values from -220 to 220
- out_gain: bfloat16 [4096], P('head'), may hold values from 0.5 to 1.5
- doc_starts: int32 [16], replicated, may hold values from 0 to 24575, as said below
Outputs:
- normed: bfloat16 [24576, 4096], P('ctx', 'head')
The draws below stay inside these ranges and needn't reach their ends.
Inputs may be any that keep to these rules, and one draw needn't show every extreme that they name: `doc_starts`: ascending and distinct, the first entry 0, the last entry 24575.
All inputs are finite; a program needn't handle non-finite values.
Results may differ from the reference program's by a relative error of at most 0.001.
Values sent between devices are 32-bit elements; how exact they have to be, the bound alone decides.
No kernel may reach another device: no remote copies, remote signals or barrier semaphores. Data moves between devices by JAX's collectives and lax.ppermute only.
A program may use at most 192 MiB of HBM per device.

```python
import math
import jax
import jax.numpy as jnp
from jax import lax

HEADS = 32
HD = 128
D = 4096
TOKENS = 24576
BLOCK = 512
NDOCS = 16


def draw_value_rows(key, part):
    first, second, third = jax.random.split(jax.random.fold_in(key, 11), 3)
    basic = jnp.clip(jax.random.normal(first, (TOKENS, HEADS, HD), jnp.float32), -6.0, 6.0)
    token_scale = jnp.exp(jax.random.uniform(third, (TOKENS,), jnp.float32, 0.0, math.log(10.0)))
    rising = math.log(3.0) * jnp.arange(HEADS, dtype=jnp.float32) / max(HEADS - 1, 1)
    head_scale = jnp.exp(rising + jax.random.uniform(second, (HEADS,), jnp.float32, 0.0, math.log(3.4)))
    scaled = basic * head_scale[None, :, None] * token_scale[:, None, None] * 0.3
    scaled = jnp.clip(scaled, -220.0, 220.0)
    return scaled.reshape(TOKENS, HEADS * HD).astype(jnp.bfloat16)


def draw_doc_starts(key, part):
    chosen = jax.random.permutation(jax.random.fold_in(key, 23), TOKENS - 2)[:NDOCS - 2] + 1
    ordered = jnp.sort(chosen.astype(jnp.int32))
    first_start = jnp.zeros((1,), jnp.int32)
    last_start = jnp.full((1,), TOKENS - 1, jnp.int32)
    return jnp.concatenate([first_start, ordered, last_start]).astype(jnp.int32)


def shard_levels(key, dims, cuts, least, top_value):
    loudness, own = 1.0, jax.random.fold_in(key, 6)
    for position, shards_of in cuts:
        draws = jnp.exp(jax.random.uniform(jax.random.fold_in(own, position), (shards_of,), jnp.float32, least / len(cuts), top_value / len(cuts)))
        loudness = loudness * jnp.repeat(draws, dims[position] // shards_of).reshape([-1 if axis == position else 1 for axis in range(len(dims))])
    return loudness


def centred(rng, extent, spread, most, cuts=(), held_as=jnp.bfloat16):
    values = jax.random.normal(rng, extent, jnp.float32) * spread
    if len(cuts) > 0:
        values = shard_levels(rng, extent, cuts, -0.22, 0.18) * values
    return jnp.clip(values, min=-most, max=most).astype(held_as)


def setup_inputs(seed: int = 0) -> dict:
    keys = jax.random.split(jax.random.key(seed), 6)
    query_rows = centred(keys[0], (TOKENS, D), 1.0, 6.0, ((0, 8), (1, 4)))
    key_rows = centred(keys[1], (TOKENS, D), 1.0, 6.0, ((0, 8), (1, 4)))
    value_rows = draw_value_rows(jax.random.fold_in(keys[5], 71), 0)
    out_gain = jnp.clip(1.0 + 0.1 * jax.random.normal(keys[3], (D,), jnp.float32), 0.5, 1.5).astype(jnp.bfloat16)
    doc_starts = draw_doc_starts(jax.random.fold_in(keys[5], 71), 0)
    return {"query_rows": query_rows, "key_rows": key_rows, "value_rows": value_rows, "out_gain": out_gain, "doc_starts": doc_starts}


def segment_of(positions, doc_starts):
    return lax.optimization_barrier(jnp.sum((doc_starts <= positions[..., None]).astype(jnp.int32), axis=-1)) - 1

def reference(query_rows, key_rows, value_rows, out_gain, doc_starts):
    tokens = query_rows.shape[0]
    block_count = tokens // BLOCK
    queries = query_rows.reshape(block_count, BLOCK, HEADS, HD)
    keyset = key_rows.reshape(block_count, BLOCK, HEADS, HD)
    valueset = value_rows.reshape(block_count, BLOCK, HEADS, HD)
    positions = jnp.arange(tokens, dtype=jnp.int32).reshape(block_count, BLOCK)
    segment = segment_of(positions, doc_starts)
    before = segment_of(positions[:, 0] - 1, doc_starts)
    causal = jnp.arange(BLOCK)[:, None] >= jnp.arange(BLOCK)[None, :]
    highest = lax.Precision.HIGHEST

    def advance(carried, items):
        query_blk, key_blk, value_blk, seg_blk, seg_before = items
        query_f = query_blk.astype(jnp.float32)
        key_f = key_blk.astype(jnp.float32)
        value_f = value_blk.astype(jnp.float32)
        scores = jnp.einsum('ihd,jhd->hij', query_f, key_f, precision=highest)
        allowed = causal & (seg_blk[:, None] == seg_blk[None, :])
        scores = jnp.where(allowed[None], scores, jnp.float32(0.0))
        within = jnp.einsum('hij,jhe->ihe', scores, value_f, precision=highest)
        across = jnp.einsum('ihd,hde->ihe', query_f, carried, precision=highest)
        live = (seg_blk == seg_before)[:, None, None]
        result = within + jnp.where(live, across, jnp.float32(0.0))
        tail_mask = (seg_blk == seg_blk[-1])[:, None, None]
        masked_keys = jnp.where(tail_mask, key_f, jnp.float32(0.0))
        contrib = jnp.einsum('ihd,ihe->hde', masked_keys, value_f, precision=highest)
        reset = seg_blk[-1] != seg_before
        carried = jnp.where(reset, contrib, carried + contrib)
        return (carried, result)
    initial = jnp.zeros((HEADS, HD, HD), jnp.float32)
    _, attended = lax.scan(advance, initial, (queries, keyset, valueset, segment, before))
    attended = attended.reshape(tokens, HEADS * HD)
    squares = lax.optimization_barrier(jnp.sum(attended * attended, axis=1, keepdims=True))
    normed = attended * lax.rsqrt(squares / (HEADS * HD) + 1e-06) * out_gain.astype(jnp.float32)[None, :]
    return normed.astype(jnp.bfloat16)
```

```python
import functools
import jax
import jax.numpy as jnp
from jax import lax
from jax.experimental import pallas as pl
from jax.experimental.pallas import tpu as pltpu
from jax.sharding import PartitionSpec as P

HEADS = 32
HD = 128
CH = 128
STEP = 512
GROUPS = 2
AHEAD = 4
bf16, f32, i32 = jnp.bfloat16, jnp.float32, jnp.int32
VM = pl.BlockSpec(memory_space=pltpu.VMEM)
SM = pl.BlockSpec(memory_space=pltpu.SMEM)
HB = pl.BlockSpec(memory_space=pltpu.HBM)


def params(mib):
    return pltpu.CompilerParams(vmem_limit_bytes=mib << 20)


def mm(a, b):
    return jnp.dot(a, b, preferred_element_type=f32)


def split(x):
    hi = x.astype(bf16)
    return hi, (x - hi.astype(f32)).astype(bf16)


def diagonal(a, b):
    zero = jnp.zeros((HD, HD), a.dtype)
    return jnp.concatenate([jnp.concatenate([a, zero], 1), jnp.concatenate([zero, b], 1)], 0)


def starts_in(starts_ref, low, high):
    count = jnp.int32(0)
    for d in range(starts_ref.shape[0]):
        count += ((starts_ref[d] >= low) & (starts_ref[d] < high)).astype(i32)
    return count


def states_kernel(col, first, starts_ref, dev_ref, k_hbm, v_hbm, q_hbm, kt_ref, v_ref, q_ref, st_ref, sum_ref, *rest):
    if first:
        mask_ref, live_ref, kbuf, sem = rest
    else:
        kbuf, sem = rest
    tokens, feats = v_ref.shape
    heads, chunks, steps, per = feats // HD, tokens // CH, tokens // STEP, STEP // CH
    copies = []
    for n, (src, dst) in enumerate(((k_hbm, kbuf), (v_hbm, v_ref), (q_hbm, q_ref))):
        copies.append([])
        for p in range(steps):
            rows = pl.ds(p * STEP, STEP)
            copies[n].append(pltpu.make_async_copy(src.at[rows, pl.ds(col, feats)], dst.at[rows], sem.at[n, p]))
    for p in range(steps):
        copies[0][p].start()
        copies[1][p].start()
    for p in range(steps):
        copies[2][p].start()
    base = lax.broadcasted_iota(i32, (chunks, CH), 0) * CH
    at = base + lax.broadcasted_iota(i32, (chunks, CH), 1)
    start = jnp.full((chunks, CH), -1, i32)
    for d in range(starts_ref.shape[0]):
        s = starts_ref[d] - dev_ref[0] * tokens
        start = jnp.where(at >= s, jnp.maximum(start, s), start)
    last = start[:, CH - 1:]
    tail = (at >= last).astype(f32)
    keep = (last < base).astype(f32)
    if first:
        rel = (start - base).astype(f32)
        row = lax.broadcasted_iota(i32, (CH, CH), 0).astype(f32)
        lane = lax.broadcasted_iota(i32, (CH, CH), 1).astype(f32)
        causal = (lane <= row).astype(f32)
        for c in range(chunks):
            lower = jnp.broadcast_to(rel[c:c + 1], (CH, CH)).T
            mask_ref[c * CH:(c + 1) * CH, :] = jnp.where(lane >= lower, causal, 0.0)
            live_ref[c * CH:(c + 1) * CH, :] = (lower < 0.0).astype(f32).astype(bf16)
    for h in range(heads):
        st_ref[0, h] = jnp.zeros((HD, HD), f32)

    def advance(c, h, added):
        s = st_ref[c, h] * keep[c:c + 1] + added
        if c + 1 < chunks:
            st_ref[c + 1, h] = s
        else:
            sum_ref[h] = s

    waiting = []
    for c in range(chunks):
        if c % per == 0:
            copies[0][c // per].wait()
            copies[1][c // per].wait()
        rows = slice(c * CH, (c + 1) * CH)
        t = tail[c:c + 1].astype(bf16)
        for h in range(heads):
            cols = slice(h * HD, (h + 1) * HD)
            kt = kbuf[rows, cols].T
            kt_ref[cols, rows] = kt
            waiting.append((c, h, mm(kt * t, v_ref[rows, cols])))
            if len(waiting) > AHEAD:
                advance(*waiting.pop(0))
    for item in waiting:
        advance(*item)
    for p in range(steps):
        copies[2][p].wait()


def states_call(col, feats, first, starts, dev, k, v, q):
    tokens = k.shape[0]
    heads, chunks, steps = feats // HD, tokens // CH, tokens // STEP
    rows = pltpu.VMEM((tokens, feats), bf16)
    out = [pltpu.VMEM((feats, tokens), bf16), rows, rows,
           pltpu.VMEM((chunks, heads, HD, HD), f32), pltpu.VMEM((heads, HD, HD), f32)]
    if first:
        out += [pltpu.VMEM((tokens, CH), f32), pltpu.VMEM((tokens, CH), bf16)]
    k, v, q = (pltpu.with_memory_space_constraint(x, pltpu.HBM) for x in (k, v, q))
    return pl.pallas_call(
        functools.partial(states_kernel, col, first), in_specs=[SM, SM, HB, HB, HB], out_specs=[VM] * len(out), out_shape=out,
        scratch_shapes=[pltpu.VMEM((tokens, feats), bf16),
                        pltpu.SemaphoreType.DMA((3, steps))],
        compiler_params=params(8), name="states")(starts, dev, k, v, q)


def within_kernel(mask_ref, q_ref, kt_ref, v_ref, o_ref):
    tokens, feats = v_ref.shape

    def finish(rows, both, a, b, hi, lo):
        vd = diagonal(v_ref[rows, a], v_ref[rows, b])
        o_ref[rows, both] = mm(hi, vd) + mm(lo, vd)

    waiting = []
    for c in range(tokens // CH):
        rows = slice(c * CH, (c + 1) * CH)
        m = mask_ref[rows, :]
        m = jnp.concatenate([m, m], 1)
        for h in range(0, feats, 2 * HD):
            both, a, b = slice(h, h + 2 * HD), slice(h, h + HD), slice(h + HD, h + 2 * HD)
            scores = mm(q_ref[rows, both], diagonal(kt_ref[a, rows], kt_ref[b, rows]))
            waiting.append((rows, both, a, b) + split(scores * m))
            if len(waiting) > AHEAD:
                finish(*waiting.pop(0))
    for item in waiting:
        finish(*item)


def within_call(mask, q, kt, v):
    return pl.pallas_call(
        within_kernel, in_specs=[VM] * 4, out_specs=VM, out_shape=pltpu.VMEM(v.shape, f32),
        compiler_params=params(8), name="within")(mask, q, kt, v)


def joined_kernel(starts_ref, dev_ref, own_ref, other_ref, o_ref):
    tokens = dev_ref[1]
    odd = dev_ref[0] % 2
    low = (dev_ref[0] - odd + 1) * tokens
    empty = (starts_in(starts_ref, low, low + tokens) == 0).astype(f32)
    one = jnp.float32(1.0)
    o_ref[...] = own_ref[...] * jnp.where(odd == 1, one, empty) + other_ref[...] * jnp.where(odd == 1, empty, one)


def joined_call(starts, dev, own, other):
    return pl.pallas_call(
        joined_kernel, in_specs=[SM, SM, VM, VM], out_specs=VM, out_shape=pltpu.VMEM(own.shape, f32),
        compiler_params=params(8), name="joined")(starts, dev, own, other)


def across_kernel(last, starts_ref, dev_ref, live_ref, q_ref, st_ref, other_ref, planes_ref, att_ref, *rest):
    if last:
        sq_in, o_ref, sq_ref, ent = rest
    else:
        o_ref, sq_ref, ent = rest
    tokens, feats = q_ref.shape
    heads = feats // HD
    dev = dev_ref[0]
    odd = dev % 2
    anchor = dev * tokens
    empty = (starts_in(starts_ref, anchor - tokens, anchor) == 0).astype(f32)
    one, zero = jnp.float32(1.0), jnp.float32(0.0)
    ent[...] = other_ref[...] * jnp.where(odd == 1, one, zero) + planes_ref[...] * jnp.where(
        dev < 2, zero, jnp.where(odd == 1, empty, one))
    first = jnp.int32(tokens)
    for d in range(starts_ref.shape[0]):
        s = starts_ref[d] - anchor
        first = jnp.where(s >= 0, jnp.minimum(first, s), first)

    totals = [None] * (tokens // CH)

    def finish(c, h, x):
        rows, cols = slice(c * CH, (c + 1) * CH), slice(h * HD, (h + 1) * HD)
        o = att_ref[rows, cols] + (x[:, :HD] + x[:, HD:])
        o_ref[rows, cols] = o
        totals[c] = o * o if h == 0 else totals[c] + o * o
        if h == heads - 1:
            line = jnp.sum(totals[c].T, axis=0, keepdims=True)
            sq_ref[c:c + 1, :] = line + sq_in[c:c + 1, :] if last else line

    waiting = []
    for c in range(tokens // CH):
        rows = slice(c * CH, (c + 1) * CH)
        lv = live_ref[rows, :]
        reach = jnp.where(c * CH <= first, one, zero)
        for h in range(heads):
            hi, lo = split(st_ref[c, h] + ent[h] * reach)
            waiting.append((c, h, mm(q_ref[rows, h * HD:(h + 1) * HD] * lv, jnp.concatenate([hi, lo], 1))))
            if len(waiting) > AHEAD:
                finish(*waiting.pop(0))
    for item in waiting:
        finish(*item)


def across_call(starts, dev, live, q, st, other, planes, att, sq=None):
    tokens, feats = att.shape
    last = sq is not None
    args = (starts, dev, live, q, st, other, planes, att) + ((sq,) if last else ())
    return pl.pallas_call(
        functools.partial(across_kernel, last), in_specs=[SM, SM] + [VM] * (len(args) - 2), out_specs=[VM, VM],
        out_shape=[pltpu.VMEM(att.shape, f32), pltpu.VMEM((tokens // CH, CH), f32)],
        scratch_shapes=[pltpu.VMEM(other.shape, f32)],
        input_output_aliases={7: 0}, compiler_params=params(8), name="across")(*args)


def norm_kernel(width, groups, *refs):
    atts, (mine_ref, theirs_ref, gain_ref, o_hbm, buf, sem) = refs[:groups], refs[groups:]
    tokens, feats = atts[0].shape
    steps, per = tokens // STEP, STEP // CH
    scale = lax.rsqrt((mine_ref[...] + theirs_ref[...]) / width + 1e-6)
    gain = gain_ref[...].astype(f32)
    copies = []
    for p in range(steps):
        for c in range(p * per, (p + 1) * per):
            rows = slice(c * CH, (c + 1) * CH)
            r = jnp.broadcast_to(scale[c:c + 1], (CH, CH)).T
            for g in range(groups):
                for h in range(feats // HD):
                    cols, place = slice(h * HD, (h + 1) * HD), slice(g * feats + h * HD, g * feats + (h + 1) * HD)
                    buf[rows, place] = (atts[g][rows, cols] * r * gain[:, place]).astype(bf16)
        rows = pl.ds(p * STEP, STEP)
        copy = pltpu.make_async_copy(buf.at[rows], o_hbm.at[rows], sem.at[p])
        copy.start()
        copies.append(copy)
    for copy in copies:
        copy.wait()


def norm_call(width, atts, mine, theirs, gain):
    tokens, feats = atts[0].shape
    groups = len(atts)
    atts = [pltpu.with_memory_space_constraint(x, pltpu.VMEM) for x in atts]
    return pl.pallas_call(
        functools.partial(norm_kernel, width, groups), in_specs=[VM] * (groups + 3), out_specs=HB,
        out_shape=pltpu.HBM((tokens, feats * groups), bf16),
        scratch_shapes=[pltpu.VMEM((tokens, feats * groups), bf16), pltpu.SemaphoreType.DMA((tokens // STEP,))],
        compiler_params=params(10), name="norm")(*atts, mine, theirs, gain)


def core(dev, hops, through, query_rows, key_rows, value_rows, out_gain, doc_starts):
    features = query_rows.shape[1]
    slabs, ways = lax.axis_size("ctx"), lax.axis_size("head")
    feats = features // GROUPS
    beside = [(i, i ^ 1) for i in range(slabs)]
    onward = [(i, i + 2) for i in range(slabs - 2)]
    states, other = [], []
    for g in range(GROUPS):
        states.append(states_call(g * feats, feats, g == 0, doc_starts, dev, key_rows, value_rows, query_rows))
        other.append(lax.ppermute(states[g][4], "ctx", beside))
    mask, live = states[0][5:]
    planes, atts = [], []
    for g in range(GROUPS):
        kt, v, q = states[g][:3]
        planes.append(lax.ppermute(joined_call(doc_starts, dev, states[g][4], other[g]), "ctx", onward))
        atts.append(within_call(mask, q, kt, v))
    sq = None
    for g in range(GROUPS):
        q, st = states[g][2:4]
        far = planes[g]
        if hops is not None:
            far = lax.fori_loop(0, hops, lambda _, p: planes[g] + through * lax.ppermute(p, "ctx", onward), far)
        atts[g], sq = across_call(doc_starts, dev, live, q, st, other[g], far, atts[g], sq)
    mine = sq
    for bit in range(ways.bit_length() - 1):
        theirs = lax.ppermute(mine, "head", [(i, i ^ (1 << bit)) for i in range(ways)])
        if bit < ways.bit_length() - 2:
            mine = mine + theirs
    return norm_call(HEADS * HD, atts, mine, theirs, out_gain.reshape(1, -1))


def shards(query_rows, key_rows, value_rows, out_gain, doc_starts):
    tokens = query_rows.shape[0]
    pairs = lax.axis_size("ctx") // 2
    me = lax.axis_index("ctx").astype(i32)
    dev = jnp.stack([me, jnp.int32(tokens)])
    plane = doc_starts // (2 * tokens)
    hops, streak = jnp.int32(0), jnp.int32(0)
    for p in range(1, pairs - 1):
        streak = jnp.where(jnp.any(plane == p), 0, streak + 1)
        hops = jnp.maximum(hops, streak)
    through = jnp.where(jnp.any(plane == me // 2 - 1), 0.0, 1.0).astype(f32)
    args = (query_rows, key_rows, value_rows, out_gain, doc_starts)
    near = core(dev, None, through, *args)
    return lax.cond(hops > 0, lambda near, *rest: core(*rest), lambda near, *rest: near, near, dev, hops, through, *args)


def solution(mesh):
    placed = (P("ctx", "head"), P("ctx", "head"), P("ctx", "head"), P("head"), P())
    return jax.shard_map(
        shards, mesh=mesh, in_specs=placed, out_specs=P("ctx", "head"), check_vma=False
    )
```

```python
import functools
import jax
import jax.numpy as jnp
from jax import lax
from jax.experimental import pallas as pl
from jax.experimental.pallas import tpu as pltpu
from jax.sharding import PartitionSpec as P

HEADS = 32
HD = 128
CH = 128
STEP = 512
GROUPS = 2
AHEAD = 4
bf16, f32, i32 = jnp.bfloat16, jnp.float32, jnp.int32
VM = pl.BlockSpec(memory_space=pltpu.VMEM)
SM = pl.BlockSpec(memory_space=pltpu.SMEM)
HB = pl.BlockSpec(memory_space=pltpu.HBM)


def params(mib):
    return pltpu.CompilerParams(vmem_limit_bytes=mib << 20)


def mm(a, b):
    return jnp.dot(a, b, preferred_element_type=f32)


def split(x):
    hi = x.astype(bf16)
    return hi, (x - hi.astype(f32)).astype(bf16)


def diagonal(a, b):
    zero = jnp.zeros((HD, HD), a.dtype)
    return jnp.concatenate([jnp.concatenate([a, zero], 1), jnp.concatenate([zero, b], 1)], 0)


def starts_in(starts_ref, low, high):
    count = jnp.int32(0)
    for d in range(starts_ref.shape[0]):
        count += ((starts_ref[d] >= low) & (starts_ref[d] < high)).astype(i32)
    return count


def states_kernel(col, first, pairs, starts_ref, dev_ref, k_hbm, v_hbm, q_hbm, kt_ref, v_ref, q_ref, st_ref, sum_ref, *rest):
    if first:
        mask_ref, live_ref, hops_ref, kbuf, sem = rest
    else:
        kbuf, sem = rest
    tokens, feats = v_ref.shape
    heads, chunks, steps, per = feats // HD, tokens // CH, tokens // STEP, STEP // CH
    copies = []
    for n, (src, dst) in enumerate(((k_hbm, kbuf), (v_hbm, v_ref), (q_hbm, q_ref))):
        copies.append([])
        for p in range(steps):
            rows = pl.ds(p * STEP, STEP)
            copies[n].append(pltpu.make_async_copy(src.at[rows, pl.ds(col, feats)], dst.at[rows], sem.at[n, p]))
    for p in range(steps):
        copies[0][p].start()
        copies[1][p].start()
    for p in range(steps):
        copies[2][p].start()
    if first:
        hops, streak, through = jnp.int32(0), jnp.int32(0), jnp.int32(1)
        for p in range(pairs):
            bare = starts_in(starts_ref, p * 2 * tokens, (p + 1) * 2 * tokens) == 0
            through = jnp.where((dev_ref[0] // 2 == p + 1) & ~bare, 0, through)
            if 0 < p < pairs - 1:
                streak = jnp.where(bare, streak + 1, 0)
                hops = jnp.maximum(hops, streak)
        hops_ref[0] = hops
        hops_ref[1] = through
    base = lax.broadcasted_iota(i32, (chunks, CH), 0) * CH
    at = base + lax.broadcasted_iota(i32, (chunks, CH), 1)
    start = jnp.full((chunks, CH), -1, i32)
    for d in range(starts_ref.shape[0]):
        s = starts_ref[d] - dev_ref[0] * tokens
        start = jnp.where(at >= s, jnp.maximum(start, s), start)
    last = start[:, CH - 1:]
    tail = (at >= last).astype(f32)
    keep = (last < base).astype(f32)
    if first:
        rel = (start - base).astype(f32)
        row = lax.broadcasted_iota(i32, (CH, CH), 0).astype(f32)
        lane = lax.broadcasted_iota(i32, (CH, CH), 1).astype(f32)
        causal = (lane <= row).astype(f32)
        for c in range(chunks):
            lower = jnp.broadcast_to(rel[c:c + 1], (CH, CH)).T
            mask_ref[c * CH:(c + 1) * CH, :] = jnp.where(lane >= lower, causal, 0.0)
            live_ref[c * CH:(c + 1) * CH, :] = (lower < 0.0).astype(f32).astype(bf16)
    for h in range(heads):
        st_ref[0, h] = jnp.zeros((HD, HD), f32)

    def advance(c, h, added):
        for i in (h, h + 1):
            s = st_ref[c, i] * keep[c:c + 1] + added[:, (i - h) * HD:(i - h + 1) * HD]
            if c + 1 < chunks:
                st_ref[c + 1, i] = s
            else:
                sum_ref[i] = s

    waiting = []
    for c in range(chunks):
        if c % per == 0:
            copies[0][c // per].wait()
            copies[1][c // per].wait()
        rows = slice(c * CH, (c + 1) * CH)
        t = tail[c:c + 1].astype(bf16)
        for h in range(0, heads, 2):
            a, b = slice(h * HD, (h + 1) * HD), slice((h + 1) * HD, (h + 2) * HD)
            ka, kb = kbuf[rows, a].T, kbuf[rows, b].T
            kt_ref[a, rows] = ka
            kt_ref[b, rows] = kb
            pair = jnp.concatenate([ka * t, kb * t], 1)
            waiting.append((c, h, mm(pair, diagonal(v_ref[rows, a], v_ref[rows, b]))))
            if len(waiting) > AHEAD:
                advance(*waiting.pop(0))
    for item in waiting:
        advance(*item)
    for p in range(steps):
        copies[2][p].wait()


def states_call(col, feats, first, pairs, starts, dev, k, v, q):
    tokens = k.shape[0]
    heads, chunks, steps = feats // HD, tokens // CH, tokens // STEP
    rows = pltpu.VMEM((tokens, feats), bf16)
    out = [pltpu.VMEM((feats, tokens), bf16), rows, rows,
           pltpu.VMEM((chunks, heads, HD, HD), f32), pltpu.VMEM((heads, HD, HD), f32)]
    if first:
        out += [pltpu.VMEM((tokens, CH), f32), pltpu.VMEM((tokens, CH), bf16), jax.ShapeDtypeStruct((2,), i32)]
    k, v, q = (pltpu.with_memory_space_constraint(x, pltpu.HBM) for x in (k, v, q))
    return pl.pallas_call(
        functools.partial(states_kernel, col, first, pairs), in_specs=[SM, SM, HB, HB, HB],
        out_specs=[VM] * 7 + [SM] if first else [VM] * 5, out_shape=out,
        scratch_shapes=[pltpu.VMEM((tokens, feats), bf16),
                        pltpu.SemaphoreType.DMA((3, steps))],
        compiler_params=params(8), name="states")(starts, dev, k, v, q)


def within_kernel(mask_ref, q_ref, kt_ref, v_ref, o_ref):
    tokens, feats = v_ref.shape

    def finish(rows, both, a, b, hi, lo):
        vd = diagonal(v_ref[rows, a], v_ref[rows, b])
        o_ref[rows, both] = mm(hi, vd) + mm(lo, vd)

    waiting = []
    for c in range(tokens // CH):
        rows = slice(c * CH, (c + 1) * CH)
        m = mask_ref[rows, :]
        m = jnp.concatenate([m, m], 1)
        for h in range(0, feats, 2 * HD):
            both, a, b = slice(h, h + 2 * HD), slice(h, h + HD), slice(h + HD, h + 2 * HD)
            scores = mm(q_ref[rows, both], diagonal(kt_ref[a, rows], kt_ref[b, rows]))
            waiting.append((rows, both, a, b) + split(scores * m))
            if len(waiting) > AHEAD:
                finish(*waiting.pop(0))
    for item in waiting:
        finish(*item)


def within_call(mask, q, kt, v):
    return pl.pallas_call(
        within_kernel, in_specs=[VM] * 4, out_specs=VM, out_shape=pltpu.VMEM(v.shape, f32),
        compiler_params=params(8), name="within")(mask, q, kt, v)


def joined_kernel(starts_ref, dev_ref, own_ref, other_ref, o_ref):
    tokens = dev_ref[1]
    odd = dev_ref[0] % 2
    low = (dev_ref[0] - odd + 1) * tokens
    empty = (starts_in(starts_ref, low, low + tokens) == 0).astype(f32)
    one = jnp.float32(1.0)
    o_ref[...] = own_ref[...] * jnp.where(odd == 1, one, empty) + other_ref[...] * jnp.where(odd == 1, empty, one)


def joined_call(starts, dev, own, other):
    return pl.pallas_call(
        joined_kernel, in_specs=[SM, SM, VM, VM], out_specs=VM, out_shape=pltpu.VMEM(own.shape, f32),
        compiler_params=params(8), name="joined")(starts, dev, own, other)


def across_kernel(last, starts_ref, dev_ref, live_ref, q_ref, st_ref, other_ref, planes_ref, att_ref, *rest):
    if last:
        sq_in, o_ref, sq_ref, ent = rest
    else:
        o_ref, sq_ref, ent = rest
    tokens, feats = q_ref.shape
    heads = feats // HD
    dev = dev_ref[0]
    odd = dev % 2
    anchor = dev * tokens
    empty = (starts_in(starts_ref, anchor - tokens, anchor) == 0).astype(f32)
    one, zero = jnp.float32(1.0), jnp.float32(0.0)
    ent[...] = other_ref[...] * jnp.where(odd == 1, one, zero) + planes_ref[...] * jnp.where(
        dev < 2, zero, jnp.where(odd == 1, empty, one))
    first = jnp.int32(tokens)
    for d in range(starts_ref.shape[0]):
        s = starts_ref[d] - anchor
        first = jnp.where(s >= 0, jnp.minimum(first, s), first)

    totals = [None] * (tokens // CH)

    def finish(c, h, x):
        rows, cols = slice(c * CH, (c + 1) * CH), slice(h * HD, (h + 2) * HD)
        o = att_ref[rows, cols] + x
        o_ref[rows, cols] = o
        o = o * o
        o = o[:, :HD] + o[:, HD:]
        totals[c] = o if h == 0 else totals[c] + o
        if h == heads - 2:
            line = jnp.sum(totals[c].T, axis=0, keepdims=True)
            sq_ref[c:c + 1, :] = line + sq_in[c:c + 1, :] if last else line

    waiting = []
    for c in range(tokens // CH):
        rows = slice(c * CH, (c + 1) * CH)
        lv = live_ref[rows, :]
        reach = jnp.where(c * CH <= first, one, zero)
        for h in range(0, heads, 2):
            x = []
            for i in (h, h + 1):
                parts = split(st_ref[c, i] + ent[i] * reach)
                y = mm(q_ref[rows, i * HD:(i + 1) * HD] * lv, jnp.concatenate(parts, 1))
                x.append(y[:, :HD] + y[:, HD:])
            waiting.append((c, h, jnp.concatenate(x, 1)))
            if len(waiting) > AHEAD:
                finish(*waiting.pop(0))
    for item in waiting:
        finish(*item)


def across_call(starts, dev, live, q, st, other, planes, att, sq=None):
    tokens, feats = att.shape
    last = sq is not None
    args = (starts, dev, live, q, st, other, planes, att) + ((sq,) if last else ())
    return pl.pallas_call(
        functools.partial(across_kernel, last), in_specs=[SM, SM] + [VM] * (len(args) - 2), out_specs=[VM, VM],
        out_shape=[pltpu.VMEM(att.shape, f32), pltpu.VMEM((tokens // CH, CH), f32)],
        scratch_shapes=[pltpu.VMEM(other.shape, f32)],
        input_output_aliases={7: 0}, compiler_params=params(8), name="across")(*args)


def norm_kernel(width, groups, *refs):
    atts, (mine_ref, theirs_ref, gain_ref, o_hbm, buf, sem) = refs[:groups], refs[groups:]
    tokens, feats = atts[0].shape
    steps, per = tokens // STEP, STEP // CH
    scale = lax.rsqrt((mine_ref[...] + theirs_ref[...]) / width + 1e-6)
    gain = gain_ref[...].astype(f32)
    copies = []
    for p in range(steps):
        for c in range(p * per, (p + 1) * per):
            rows = slice(c * CH, (c + 1) * CH)
            r = jnp.broadcast_to(scale[c:c + 1], (CH, CH)).T
            for g in range(groups):
                for h in range(feats // HD):
                    cols, place = slice(h * HD, (h + 1) * HD), slice(g * feats + h * HD, g * feats + (h + 1) * HD)
                    buf[rows, place] = (atts[g][rows, cols] * r * gain[:, place]).astype(bf16)
        rows = pl.ds(p * STEP, STEP)
        copy = pltpu.make_async_copy(buf.at[rows], o_hbm.at[rows], sem.at[p])
        copy.start()
        copies.append(copy)
    for copy in copies:
        copy.wait()


def norm_call(width, atts, mine, theirs, gain):
    tokens, feats = atts[0].shape
    groups = len(atts)
    atts = [pltpu.with_memory_space_constraint(x, pltpu.VMEM) for x in atts]
    return pl.pallas_call(
        functools.partial(norm_kernel, width, groups), in_specs=[VM] * (groups + 3), out_specs=HB,
        out_shape=pltpu.HBM((tokens, feats * groups), bf16),
        scratch_shapes=[pltpu.VMEM((tokens, feats * groups), bf16), pltpu.SemaphoreType.DMA((tokens // STEP,))],
        compiler_params=params(10), name="norm")(*atts, mine, theirs, gain)


def core(general, dev, query_rows, key_rows, value_rows, out_gain, doc_starts):
    features = query_rows.shape[1]
    slabs, ways = lax.axis_size("ctx"), lax.axis_size("head")
    feats = features // GROUPS
    beside = [(i, i ^ 1) for i in range(slabs)]
    onward = [(i, i + 2) for i in range(slabs - 2)]
    states, other = [], []
    for g in range(GROUPS):
        states.append(states_call(g * feats, feats, g == 0, slabs // 2, doc_starts, dev, key_rows, value_rows, query_rows))
        other.append(lax.ppermute(states[g][4], "ctx", beside))
    mask, live, hops = states[0][5:]
    planes, atts = [], []
    for g in range(GROUPS):
        kt, v, q = states[g][:3]
        atts.append(within_call(mask, q, kt, v))
        if g == 0:
            other[g], atts[g] = lax.optimization_barrier((other[g], atts[g]))
        planes.append(lax.ppermute(joined_call(doc_starts, dev, states[g][4], other[g]), "ctx", onward))
    sq = None
    for g in range(GROUPS):
        q, st = states[g][2:4]
        far = planes[g]
        if general:
            through = hops[1].astype(f32)
            far = lax.fori_loop(0, hops[0], lambda _, p: planes[g] + through * lax.ppermute(p, "ctx", onward), far)
        atts[g], sq = across_call(doc_starts, dev, live, q, st, other[g], far, atts[g], sq)
    mine = sq
    for bit in range(ways.bit_length() - 1):
        theirs = lax.ppermute(mine, "head", [(i, i ^ (1 << bit)) for i in range(ways)])
        if bit < ways.bit_length() - 2:
            mine = mine + theirs
    return norm_call(HEADS * HD, atts, mine, theirs, out_gain.reshape(1, -1)), hops


def shards(query_rows, key_rows, value_rows, out_gain, doc_starts):
    tokens = query_rows.shape[0]
    dev = jnp.stack([lax.axis_index("ctx").astype(i32), jnp.int32(tokens)])
    args = (dev, query_rows, key_rows, value_rows, out_gain, doc_starts)
    near, hops = core(False, *args)
    return lax.cond(hops[0] > 0, lambda near, *args: core(True, *args)[0], lambda near, *args: near, near, *args)


def solution(mesh):
    placed = (P("ctx", "head"), P("ctx", "head"), P("ctx", "head"), P("head"), P())
    return jax.shard_map(
        shards, mesh=mesh, in_specs=placed, out_specs=P("ctx", "head"), check_vma=False
    )
```

```python
import functools
import jax
import jax.numpy as jnp
from jax import lax
from jax.experimental import pallas as pl
from jax.experimental.pallas import tpu as pltpu
from jax.sharding import PartitionSpec as P

HEADS = 32
HD = 128
CH = 128
STEP = 512
GROUPS = 2
AHEAD = 2
bf16, f32, i32 = jnp.bfloat16, jnp.float32, jnp.int32
VM = pl.BlockSpec(memory_space=pltpu.VMEM)
SM = pl.BlockSpec(memory_space=pltpu.SMEM)
HB = pl.BlockSpec(memory_space=pltpu.HBM)


def params(mib):
    return pltpu.CompilerParams(vmem_limit_bytes=mib << 20)


def mm(a, b):
    return jnp.dot(a, b, preferred_element_type=f32)


def split(x):
    hi = x.astype(bf16)
    return hi, (x - hi.astype(f32)).astype(bf16)


def diagonal(a, b):
    zero = jnp.zeros((HD, HD), a.dtype)
    return jnp.concatenate([jnp.concatenate([a, zero], 1), jnp.concatenate([zero, b], 1)], 0)


def starts_in(starts_ref, low, high):
    count = jnp.int32(0)
    for d in range(starts_ref.shape[0]):
        count += ((starts_ref[d] >= low) & (starts_ref[d] < high)).astype(i32)
    return count


def states_kernel(col, first, pairs, starts_ref, dev_ref, k_hbm, v_hbm, kt_ref, v_ref, st_ref, sum_ref, *rest):
    if first:
        mask_ref, live_ref, hops_ref, kbuf, sem = rest
    else:
        kbuf, sem = rest
    tokens, feats = v_ref.shape
    heads, chunks, steps, per = feats // HD, tokens // CH, tokens // STEP, STEP // CH
    copies = []
    for p in range(steps):
        rows = pl.ds(p * STEP, STEP)
        copies.append([pltpu.make_async_copy(src.at[rows, pl.ds(col, feats)], dst.at[rows], sem.at[n, p])
                       for n, (src, dst) in enumerate(((k_hbm, kbuf), (v_hbm, v_ref)))])
        for copy in copies[p]:
            copy.start()
    if first:
        hops, streak, through = jnp.int32(0), jnp.int32(0), jnp.int32(1)
        for p in range(pairs):
            bare = starts_in(starts_ref, p * 2 * tokens, (p + 1) * 2 * tokens) == 0
            through = jnp.where((dev_ref[0] // 2 == p + 1) & ~bare, 0, through)
            if 0 < p < pairs - 1:
                streak = jnp.where(bare, streak + 1, 0)
                hops = jnp.maximum(hops, streak)
        hops_ref[0] = hops
        hops_ref[1] = through
    base = lax.broadcasted_iota(i32, (chunks, CH), 0) * CH
    at = base + lax.broadcasted_iota(i32, (chunks, CH), 1)
    start = jnp.full((chunks, CH), -1, i32)
    for d in range(starts_ref.shape[0]):
        s = starts_ref[d] - dev_ref[0] * tokens
        start = jnp.where(at >= s, jnp.maximum(start, s), start)
    last = start[:, CH - 1:]
    tail = (at >= last).astype(f32)
    keep = (last < base).astype(f32)
    if first:
        rel = (start - base).astype(f32)
        row = lax.broadcasted_iota(i32, (CH, CH), 0).astype(f32)
        lane = lax.broadcasted_iota(i32, (CH, CH), 1).astype(f32)
        causal = (lane <= row).astype(f32)
        for c in range(chunks):
            lower = jnp.broadcast_to(rel[c:c + 1], (CH, CH)).T
            mask_ref[c * CH:(c + 1) * CH, :] = jnp.where(lane >= lower, causal, 0.0)
            live_ref[c * CH:(c + 1) * CH, :] = (lower < 0.0).astype(f32).astype(bf16)
    st_ref[0] = jnp.zeros(st_ref.shape[1:], f32)

    def advance(c, h, added):
        for i in (h, h + 1):
            s = st_ref[c, i] * keep[c:c + 1] + added[:, (i - h) * HD:(i - h + 1) * HD]
            if c + 1 < chunks:
                st_ref[c + 1, i] = s
            else:
                sum_ref[i] = s

    waiting = []
    for c in range(chunks):
        if c % per == 0:
            for copy in copies[c // per]:
                copy.wait()
        rows = slice(c * CH, (c + 1) * CH)
        t = tail[c:c + 1].astype(bf16)
        for h in range(0, heads, 2):
            a, b = slice(h * HD, (h + 1) * HD), slice((h + 1) * HD, (h + 2) * HD)
            ka, kb = kbuf[rows, a].T, kbuf[rows, b].T
            kt_ref[a, rows] = ka
            kt_ref[b, rows] = kb
            pair = jnp.concatenate([ka * t, kb * t], 1)
            waiting.append((c, h, mm(pair, diagonal(v_ref[rows, a], v_ref[rows, b]))))
            if len(waiting) > AHEAD:
                advance(*waiting.pop(0))
    for item in waiting:
        advance(*item)

def states_call(col, feats, first, pairs, starts, dev, k, v):
    tokens = k.shape[0]
    heads, chunks, steps = feats // HD, tokens // CH, tokens // STEP
    k, v = (pltpu.with_memory_space_constraint(x, pltpu.HBM) for x in (k, v))
    out = [pltpu.VMEM((feats, tokens), bf16), pltpu.VMEM((tokens, feats), bf16),
           pltpu.VMEM((chunks, heads, HD, HD), f32), pltpu.VMEM((heads, HD, HD), f32)]
    if first:
        out += [pltpu.VMEM((tokens, CH), f32), pltpu.VMEM((tokens, CH), bf16), jax.ShapeDtypeStruct((2,), i32)]
    return pl.pallas_call(
        functools.partial(states_kernel, col, first, pairs), in_specs=[SM, SM, HB, HB],
        out_specs=[VM] * 6 + [SM] if first else [VM] * 4, out_shape=out,
        scratch_shapes=[pltpu.VMEM((tokens, feats), bf16), pltpu.SemaphoreType.DMA((2, steps))],
        compiler_params=params(8), name="states")(starts, dev, k, v)


def within_kernel(col, mask_ref, q_ref, kt_ref, v_ref, o_ref):
    tokens, feats = o_ref.shape

    def finish(rows, h, hi, lo):
        vd = diagonal(v_ref[rows, h:h + HD], v_ref[rows, h + HD:h + 2 * HD])
        o_ref[rows, h:h + 2 * HD] = mm(hi, vd) + mm(lo, vd)

    waiting = []
    for c in range(tokens // CH):
        rows = slice(c * CH, (c + 1) * CH)
        m = mask_ref[rows, :]
        m = jnp.concatenate([m, m], 1)
        for h in range(0, feats, 2 * HD):
            kd = diagonal(kt_ref[h:h + HD, rows], kt_ref[h + HD:h + 2 * HD, rows])
            waiting.append((rows, h) + split(mm(q_ref[rows, col + h:col + h + 2 * HD], kd) * m))
            if len(waiting) > AHEAD:
                finish(*waiting.pop(0))
    for item in waiting:
        finish(*item)


def within_call(col, feats, mask, q, kt, v):
    tokens = v.shape[0]
    return pl.pallas_call(
        functools.partial(within_kernel, col), in_specs=[VM] * 4, out_specs=VM, out_shape=pltpu.VMEM((tokens, feats), f32),
        compiler_params=params(8), name="within")(mask, q, kt, v)


def joined_kernel(starts_ref, dev_ref, own_ref, other_ref, o_ref):
    tokens = dev_ref[1]
    odd = dev_ref[0] % 2
    low = (dev_ref[0] - odd + 1) * tokens
    empty = (starts_in(starts_ref, low, low + tokens) == 0).astype(f32)
    one = jnp.float32(1.0)
    o_ref[...] = own_ref[...] * jnp.where(odd == 1, one, empty) + other_ref[...] * jnp.where(odd == 1, empty, one)


def joined_call(starts, dev, own, other):
    return pl.pallas_call(
        joined_kernel, in_specs=[SM, SM, VM, VM], out_specs=VM, out_shape=pltpu.VMEM(own.shape, f32),
        compiler_params=params(8), name="joined")(starts, dev, own, other)


def across_kernel(last, head, starts_ref, dev_ref, live_ref, q_ref, st_ref, other_ref, att_ref, odd_ref, even_ref, *rest):
    if last:
        sq_in, o_ref, sq_ref, ent = rest
    else:
        o_ref, sq_ref, ent = rest
    tokens, feats = att_ref.shape
    heads = feats // HD
    dev = dev_ref[0]
    odd = dev % 2
    anchor = dev * tokens
    empty = (starts_in(starts_ref, anchor - tokens, anchor) == 0).astype(f32)
    one, zero = jnp.float32(1.0), jnp.float32(0.0)
    ent[1] = jnp.zeros(ent.shape[1:], f32)
    plane = jnp.where(dev < 2, zero, jnp.where(odd == 1, empty, one))
    second = dev // 2 % 2 == 1
    ent[0] = (other_ref[...] * jnp.where(odd == 1, one, zero) + odd_ref[...] * jnp.where(second, plane, zero)
              + even_ref[...] * jnp.where(second, zero, plane))
    first = jnp.int32(tokens)
    for d in range(starts_ref.shape[0]):
        s = starts_ref[d] - anchor
        first = jnp.where(s >= 0, jnp.minimum(first, s), first)

    totals = [None] * (tokens // CH)

    def finish(c, h, x):
        rows, cols = slice(c * CH, (c + 1) * CH), slice(h * HD, (h + 2) * HD)
        o = att_ref[rows, cols] + x
        o_ref[rows, cols] = o
        o = o * o
        o = o[:, :HD] + o[:, HD:]
        totals[c] = o if h == 0 else totals[c] + o
        if h == heads - 2:
            line = jnp.sum(totals[c].T, axis=0, keepdims=True)
            sq_ref[c:c + 1, :] = line + sq_in[c:c + 1, :] if last else line

    waiting = []
    for c in range(tokens // CH):
        rows = slice(c * CH, (c + 1) * CH)
        lv = live_ref[rows, :]
        gone = (c * CH > first).astype(i32)
        for h in range(0, heads, 2):
            x = []
            for i in (h, h + 1):
                parts = split(st_ref[c, i] + ent[gone, i])
                y = mm(q_ref[rows, (head + i) * HD:(head + i + 1) * HD] * lv, jnp.concatenate(parts, 1))
                x.append(y[:, :HD] + y[:, HD:])
            waiting.append((c, h, jnp.concatenate(x, 1)))
            if len(waiting) > AHEAD:
                finish(*waiting.pop(0))
    for item in waiting:
        finish(*item)


def across_call(head, starts, dev, live, q, st, other, planes, att, sq=None):
    tokens, feats = att.shape
    last = sq is not None
    args = (starts, dev, live, q, st, other, att, *planes) + ((sq,) if last else ())
    return pl.pallas_call(
        functools.partial(across_kernel, last, head), in_specs=[SM, SM] + [VM] * (len(args) - 2), out_specs=[VM, VM],
        out_shape=[pltpu.VMEM(att.shape, f32), pltpu.VMEM((tokens // CH, CH), f32)],
        scratch_shapes=[pltpu.VMEM((2,) + other.shape, f32)],
        input_output_aliases={6: 0}, compiler_params=params(8), name="across")(*args)


def norm_kernel(width, groups, *refs):
    atts, (mine_ref, theirs_ref, gain_ref, o_hbm, buf, sem) = refs[:groups], refs[groups:]
    tokens, feats = atts[0].shape
    steps, per = tokens // STEP, STEP // CH
    scale = lax.rsqrt((mine_ref[...] + theirs_ref[...]) / width + 1e-6)
    gain = gain_ref[...].astype(f32)
    copies = []
    for p in range(steps):
        for c in range(p * per, (p + 1) * per):
            rows = slice(c * CH, (c + 1) * CH)
            r = jnp.broadcast_to(scale[c:c + 1], (CH, CH)).T
            for g in range(groups):
                for h in range(feats // HD):
                    cols, place = slice(h * HD, (h + 1) * HD), slice(g * feats + h * HD, g * feats + (h + 1) * HD)
                    buf[rows, place] = (atts[g][rows, cols] * r * gain[:, place]).astype(bf16)
        rows = pl.ds(p * STEP, STEP)
        copy = pltpu.make_async_copy(buf.at[rows], o_hbm.at[rows], sem.at[p])
        copy.start()
        copies.append(copy)
    for copy in copies:
        copy.wait()


def norm_call(width, atts, mine, theirs, gain):
    tokens, feats = atts[0].shape
    groups = len(atts)
    atts = [pltpu.with_memory_space_constraint(x, pltpu.VMEM) for x in atts]
    return pl.pallas_call(
        functools.partial(norm_kernel, width, groups), in_specs=[VM] * (groups + 3), out_specs=HB,
        out_shape=pltpu.HBM((tokens, feats * groups), bf16),
        scratch_shapes=[pltpu.VMEM((tokens, feats * groups), bf16), pltpu.SemaphoreType.DMA((tokens // STEP,))],
        compiler_params=params(8), name="norm")(*atts, mine, theirs, gain)


def core(general, dev, query_rows, key_rows, value_rows, out_gain, doc_starts):
    features = query_rows.shape[1]
    slabs, ways = lax.axis_size("ctx"), lax.axis_size("head")
    feats = features // GROUPS
    beside = [(i, i ^ 1) for i in range(slabs)]
    onward = [(i, i + 2) for i in range(slabs - 2)]
    both = ("ctx", "head")

    def swaps(odd):
        to = []
        for me in range(slabs * ways):
            p = me // (2 * ways)
            mate = p + 1 if p % 2 == odd else p - 1
            to.append((me, me + (mate - p) * 2 * ways if 0 <= mate < slabs // 2 else me ^ 1))
        return to

    states, other = [], []
    for g in range(GROUPS):
        states.append(states_call(g * feats, feats, g == 0, slabs // 2, doc_starts, dev, key_rows, value_rows))
        other.append(lax.ppermute(states[g][3], "ctx", beside))
    mask, live, hops = states[0][4:]
    queries = pltpu.with_memory_space_constraint(query_rows, pltpu.VMEM)
    planes, atts = [], []
    for g in range(GROUPS):
        atts.append(within_call(g * feats, feats, mask, queries, *states[g][:2]))
        if g == 0:
            other[g], atts[g] = lax.optimization_barrier((other[g], atts[g]))
        joined = joined_call(doc_starts, dev, states[g][3], other[g])
        planes.append([lax.ppermute(joined, both, swaps(odd)) for odd in (0, 1)])
    sq = None
    for g in range(GROUPS):
        far = planes[g]
        if general:
            through = hops[1].astype(f32)
            near = jnp.where(dev[0] // 2 % 2 == 1, far[0], far[1]) * jnp.where(dev[0] < 2, 0.0, 1.0)
            far = [lax.fori_loop(0, hops[0], lambda _, p: near + through * lax.ppermute(p, "ctx", onward), near)] * 2
        atts[g], sq = across_call(g * feats // HD, doc_starts, dev, live, queries, states[g][2], other[g], far, atts[g], sq)
    mine = sq
    for bit in range(ways.bit_length() - 1):
        theirs = lax.ppermute(mine, "head", [(i, i ^ (1 << bit)) for i in range(ways)])
        if bit < ways.bit_length() - 2:
            mine = mine + theirs
    return norm_call(HEADS * HD, atts, mine, theirs, out_gain.reshape(1, -1)), hops


def shards(query_rows, key_rows, value_rows, out_gain, doc_starts):
    tokens = query_rows.shape[0]
    dev = jnp.stack([lax.axis_index("ctx").astype(i32), jnp.int32(tokens)])
    args = (dev, query_rows, key_rows, value_rows, out_gain, doc_starts)
    near, hops = core(False, *args)
    return lax.cond(hops[0] > 0, lambda near, *args: core(True, *args)[0], lambda near, *args: near, near, *args)


def solution(mesh):
    placed = (P("ctx", "head"), P("ctx", "head"), P("ctx", "head"), P("head"), P())
    return jax.shard_map(
        shards, mesh=mesh, in_specs=placed, out_specs=P("ctx", "head"), check_vma=False
    )
```

```python
import functools
import jax
import jax.numpy as jnp
from jax import lax
from jax.experimental import pallas as pl
from jax.experimental.pallas import tpu as pltpu
from jax.sharding import PartitionSpec as P

HEADS = 32
HD = 128
CH = 128
STEP = 512
GROUPS = 2
AHEAD = 2
bf16, f32, i32 = jnp.bfloat16, jnp.float32, jnp.int32
VM = pl.BlockSpec(memory_space=pltpu.VMEM)
SM = pl.BlockSpec(memory_space=pltpu.SMEM)
HB = pl.BlockSpec(memory_space=pltpu.HBM)


def params(mib):
    return pltpu.CompilerParams(vmem_limit_bytes=mib << 20)


def mm(a, b):
    return jnp.dot(a, b, preferred_element_type=f32)


def split(x):
    hi = x.astype(bf16)
    return hi, (x - hi.astype(f32)).astype(bf16)


def diagonal(a, b):
    zero = jnp.zeros((HD, HD), a.dtype)
    return jnp.concatenate([jnp.concatenate([a, zero], 1), jnp.concatenate([zero, b], 1)], 0)


def starts_in(starts_ref, low, high):
    count = jnp.int32(0)
    for d in range(starts_ref.shape[0]):
        count += ((starts_ref[d] >= low) & (starts_ref[d] < high)).astype(i32)
    return count


def states_kernel(col, first, pairs, starts_ref, dev_ref, k_hbm, v_hbm, kt_ref, v_ref, st_ref, sum_ref, *rest):
    if first:
        mask_ref, live_ref, shares_ref, hops_ref, kbuf, sem = rest
    else:
        kbuf, sem = rest
    tokens, feats = v_ref.shape
    heads, chunks, steps, per = feats // HD, tokens // CH, tokens // STEP, STEP // CH
    copies = []
    for p in range(steps):
        rows = pl.ds(p * STEP, STEP)
        copies.append([pltpu.make_async_copy(src.at[rows, pl.ds(col, feats)], dst.at[rows], sem.at[n, p])
                       for n, (src, dst) in enumerate(((k_hbm, kbuf), (v_hbm, v_ref)))])
        for copy in copies[p]:
            copy.start()
    if first:
        hops, streak, through = jnp.int32(0), jnp.int32(0), jnp.int32(1)
        for p in range(pairs):
            bare = starts_in(starts_ref, p * 2 * tokens, (p + 1) * 2 * tokens) == 0
            through = jnp.where((dev_ref[0] // 2 == p + 1) & ~bare, 0, through)
            if 0 < p < pairs - 1:
                streak = jnp.where(bare, streak + 1, 0)
                hops = jnp.maximum(hops, streak)
        odd = dev_ref[0] % 2
        low = (dev_ref[0] - odd + 1) * tokens
        empty = (starts_in(starts_ref, low, low + tokens) == 0).astype(f32)
        one = jnp.float32(1.0)
        mine, theirs = jnp.where(odd == 1, one, empty), jnp.where(odd == 1, empty, one)
        shares_ref[...] = jnp.where(lax.broadcasted_iota(i32, shares_ref.shape, 0) == 0, mine, theirs)
        hops_ref[0] = hops
        hops_ref[1] = through
    base = lax.broadcasted_iota(i32, (chunks, CH), 0) * CH
    at = base + lax.broadcasted_iota(i32, (chunks, CH), 1)
    start = jnp.full((chunks, CH), -1, i32)
    for d in range(starts_ref.shape[0]):
        s = starts_ref[d] - dev_ref[0] * tokens
        start = jnp.where(at >= s, jnp.maximum(start, s), start)
    last = start[:, CH - 1:]
    tail = (at >= last).astype(f32)
    keep = (last < base).astype(f32)
    if first:
        rel = (start - base).astype(f32)
        row = lax.broadcasted_iota(i32, (CH, CH), 0).astype(f32)
        lane = lax.broadcasted_iota(i32, (CH, CH), 1).astype(f32)
        causal = (lane <= row).astype(f32)
        for c in range(chunks):
            lower = jnp.broadcast_to(rel[c:c + 1], (CH, CH)).T
            mask_ref[c * CH:(c + 1) * CH, :] = jnp.where(lane >= lower, causal, 0.0)
            live_ref[c * CH:(c + 1) * CH, :] = (lower < 0.0).astype(f32).astype(bf16)
    st_ref[0] = jnp.zeros(st_ref.shape[1:], f32)

    def advance(c, h, added):
        for i in (h, h + 1):
            s = st_ref[c, i] * keep[c:c + 1] + added[:, (i - h) * HD:(i - h + 1) * HD]
            if c + 1 < chunks:
                st_ref[c + 1, i] = s
            else:
                sum_ref[i] = s

    waiting = []
    for c in range(chunks):
        if c % per == 0:
            for copy in copies[c // per]:
                copy.wait()
        rows = slice(c * CH, (c + 1) * CH)
        t = tail[c:c + 1].astype(bf16)
        for h in range(0, heads, 2):
            a, b = slice(h * HD, (h + 1) * HD), slice((h + 1) * HD, (h + 2) * HD)
            ka, kb = kbuf[rows, a].T, kbuf[rows, b].T
            kt_ref[a, rows] = ka
            kt_ref[b, rows] = kb
            pair = jnp.concatenate([ka * t, kb * t], 1)
            waiting.append((c, h, mm(pair, diagonal(v_ref[rows, a], v_ref[rows, b]))))
            if len(waiting) > AHEAD:
                advance(*waiting.pop(0))
    for item in waiting:
        advance(*item)

def states_call(col, feats, first, pairs, starts, dev, k, v):
    tokens = k.shape[0]
    heads, chunks, steps = feats // HD, tokens // CH, tokens // STEP
    k, v = (pltpu.with_memory_space_constraint(x, pltpu.HBM) for x in (k, v))
    out = [pltpu.VMEM((feats, tokens), bf16), pltpu.VMEM((tokens, feats), bf16),
           pltpu.VMEM((chunks, heads, HD, HD), f32), pltpu.VMEM((heads, HD, HD), f32)]
    if first:
        out += [pltpu.VMEM((tokens, CH), f32), pltpu.VMEM((tokens, CH), bf16), pltpu.VMEM((8, CH), f32),
                jax.ShapeDtypeStruct((2,), i32)]
    return pl.pallas_call(
        functools.partial(states_kernel, col, first, pairs), in_specs=[SM, SM, HB, HB],
        out_specs=[VM] * 7 + [SM] if first else [VM] * 4, out_shape=out,
        scratch_shapes=[pltpu.VMEM((tokens, feats), bf16), pltpu.SemaphoreType.DMA((2, steps))],
        compiler_params=params(8), name="states")(starts, dev, k, v)


def within_kernel(col, mask_ref, q_ref, kt_ref, v_ref, o_ref):
    tokens, feats = o_ref.shape

    def finish(rows, h, hi, lo):
        vd = diagonal(v_ref[rows, h:h + HD], v_ref[rows, h + HD:h + 2 * HD])
        o_ref[rows, h:h + 2 * HD] = mm(hi, vd) + mm(lo, vd)

    waiting = []
    for c in range(tokens // CH):
        rows = slice(c * CH, (c + 1) * CH)
        m = mask_ref[rows, :]
        m = jnp.concatenate([m, m], 1)
        for h in range(0, feats, 2 * HD):
            kd = diagonal(kt_ref[h:h + HD, rows], kt_ref[h + HD:h + 2 * HD, rows])
            waiting.append((rows, h) + split(mm(q_ref[rows, col + h:col + h + 2 * HD], kd) * m))
            if len(waiting) > AHEAD:
                finish(*waiting.pop(0))
    for item in waiting:
        finish(*item)


def within_call(col, feats, mask, q, kt, v):
    tokens = v.shape[0]
    return pl.pallas_call(
        functools.partial(within_kernel, col), in_specs=[VM] * 4, out_specs=VM, out_shape=pltpu.VMEM((tokens, feats), f32),
        compiler_params=params(8), name="within")(mask, q, kt, v)


def joined_kernel(shares_ref, own_ref, other_ref, o_ref):
    o_ref[...] = own_ref[...] * shares_ref[0:1, :] + other_ref[...] * shares_ref[1:2, :]


def joined_call(shares, own, other):
    return pl.pallas_call(
        joined_kernel, in_specs=[VM] * 3, out_specs=VM, out_shape=pltpu.VMEM(own.shape, f32),
        compiler_params=params(8), name="joined")(shares, own, other)


def across_kernel(last, head, starts_ref, dev_ref, live_ref, q_ref, st_ref, other_ref, att_ref, odd_ref, even_ref, *rest):
    if last:
        sq_in, o_ref, sq_ref, ent = rest
    else:
        o_ref, sq_ref, ent = rest
    tokens, feats = att_ref.shape
    heads = feats // HD
    dev = dev_ref[0]
    odd = dev % 2
    anchor = dev * tokens
    empty = (starts_in(starts_ref, anchor - tokens, anchor) == 0).astype(f32)
    one, zero = jnp.float32(1.0), jnp.float32(0.0)
    ent[1] = jnp.zeros(ent.shape[1:], f32)
    plane = jnp.where(dev < 2, zero, jnp.where(odd == 1, empty, one))
    second = dev // 2 % 2 == 1
    ent[0] = (other_ref[...] * jnp.where(odd == 1, one, zero) + odd_ref[...] * jnp.where(second, plane, zero)
              + even_ref[...] * jnp.where(second, zero, plane))
    first = jnp.int32(tokens)
    for d in range(starts_ref.shape[0]):
        s = starts_ref[d] - anchor
        first = jnp.where(s >= 0, jnp.minimum(first, s), first)

    totals = [None] * (tokens // CH)

    def finish(c, h, x):
        rows, cols = slice(c * CH, (c + 1) * CH), slice(h * HD, (h + 2) * HD)
        o = att_ref[rows, cols] + x
        o_ref[rows, cols] = o
        o = o * o
        o = o[:, :HD] + o[:, HD:]
        totals[c] = o if h == 0 else totals[c] + o
        if h == heads - 2:
            line = jnp.sum(totals[c].T, axis=0, keepdims=True)
            sq_ref[c:c + 1, :] = line + sq_in[c:c + 1, :] if last else line

    waiting = []
    for c in range(tokens // CH):
        rows = slice(c * CH, (c + 1) * CH)
        lv = live_ref[rows, :]
        gone = (c * CH > first).astype(i32)
        for h in range(0, heads, 2):
            x = []
            for i in (h, h + 1):
                parts = split(st_ref[c, i] + ent[gone, i])
                y = mm(q_ref[rows, (head + i) * HD:(head + i + 1) * HD] * lv, jnp.concatenate(parts, 1))
                x.append(y[:, :HD] + y[:, HD:])
            waiting.append((c, h, jnp.concatenate(x, 1)))
            if len(waiting) > AHEAD:
                finish(*waiting.pop(0))
    for item in waiting:
        finish(*item)


def across_call(head, starts, dev, live, q, st, other, planes, att, sq=None):
    tokens, feats = att.shape
    last = sq is not None
    args = (starts, dev, live, q, st, other, att, *planes) + ((sq,) if last else ())
    return pl.pallas_call(
        functools.partial(across_kernel, last, head), in_specs=[SM, SM] + [VM] * (len(args) - 2), out_specs=[VM, VM],
        out_shape=[pltpu.VMEM(att.shape, f32), pltpu.VMEM((tokens // CH, CH), f32)],
        scratch_shapes=[pltpu.VMEM((2,) + other.shape, f32)],
        input_output_aliases={6: 0}, compiler_params=params(8), name="across")(*args)


def norm_kernel(width, groups, *refs):
    atts, (mine_ref, theirs_ref, gain_ref, o_hbm, buf, sem) = refs[:groups], refs[groups:]
    tokens, feats = atts[0].shape
    steps, per = tokens // STEP, STEP // CH
    scale = lax.rsqrt((mine_ref[...] + theirs_ref[...]) / width + 1e-6)
    gain = gain_ref[...].astype(f32)
    copies = []
    for p in range(steps):
        for c in range(p * per, (p + 1) * per):
            rows = slice(c * CH, (c + 1) * CH)
            r = jnp.broadcast_to(scale[c:c + 1], (CH, CH)).T
            for g in range(groups):
                for h in range(feats // HD):
                    cols, place = slice(h * HD, (h + 1) * HD), slice(g * feats + h * HD, g * feats + (h + 1) * HD)
                    buf[rows, place] = (atts[g][rows, cols] * r * gain[:, place]).astype(bf16)
        rows = pl.ds(p * STEP, STEP)
        copy = pltpu.make_async_copy(buf.at[rows], o_hbm.at[rows], sem.at[p])
        copy.start()
        copies.append(copy)
    for copy in copies:
        copy.wait()


def norm_call(width, atts, mine, theirs, gain):
    tokens, feats = atts[0].shape
    groups = len(atts)
    atts = [pltpu.with_memory_space_constraint(x, pltpu.VMEM) for x in atts]
    return pl.pallas_call(
        functools.partial(norm_kernel, width, groups), in_specs=[VM] * (groups + 3), out_specs=HB,
        out_shape=pltpu.HBM((tokens, feats * groups), bf16),
        scratch_shapes=[pltpu.VMEM((tokens, feats * groups), bf16), pltpu.SemaphoreType.DMA((tokens // STEP,))],
        compiler_params=params(8), name="norm")(*atts, mine, theirs, gain)


def core(general, dev, query_rows, key_rows, value_rows, out_gain, doc_starts):
    features = query_rows.shape[1]
    slabs, ways = lax.axis_size("ctx"), lax.axis_size("head")
    feats = features // GROUPS
    beside = [(i, i ^ 1) for i in range(slabs)]
    onward = [(i, i + 2) for i in range(slabs - 2)]
    both = ("ctx", "head")

    def swaps(odd):
        to = []
        for me in range(slabs * ways):
            p = me // (2 * ways)
            mate = p + 1 if p % 2 == odd else p - 1
            to.append((me, me + (mate - p) * 2 * ways if 0 <= mate < slabs // 2 else me ^ 1))
        return to

    states, other = [], []
    for g in range(GROUPS):
        states.append(states_call(g * feats, feats, g == 0, slabs // 2, doc_starts, dev, key_rows, value_rows))
        other.append(lax.ppermute(states[g][3], "ctx", beside))
    mask, live, shares, hops = states[0][4:]
    queries = pltpu.with_memory_space_constraint(query_rows, pltpu.VMEM)
    planes, atts = [], []
    for g in range(GROUPS):
        atts.append(within_call(g * feats, feats, mask, queries, *states[g][:2]))
        if g == 0:
            other[g], atts[g] = lax.optimization_barrier((other[g], atts[g]))
        joined = joined_call(shares, states[g][3], other[g])
        planes.append([lax.ppermute(joined, both, swaps(odd)) for odd in (0, 1)])
    sq = None
    for g in range(GROUPS):
        far = planes[g]
        if general:
            through = hops[1].astype(f32)
            near = jnp.where(dev[0] // 2 % 2 == 1, far[0], far[1]) * jnp.where(dev[0] < 2, 0.0, 1.0)
            far = [lax.fori_loop(0, hops[0], lambda _, p: near + through * lax.ppermute(p, "ctx", onward), near)] * 2
        atts[g], sq = across_call(g * feats // HD, doc_starts, dev, live, queries, states[g][2], other[g], far, atts[g], sq)
    mine = sq
    for bit in range(ways.bit_length() - 1):
        theirs = lax.ppermute(mine, "head", [(i, i ^ (1 << bit)) for i in range(ways)])
        if bit < ways.bit_length() - 2:
            mine = mine + theirs
    return norm_call(HEADS * HD, atts, mine, theirs, out_gain.reshape(1, -1)), hops


def shards(query_rows, key_rows, value_rows, out_gain, doc_starts):
    tokens = query_rows.shape[0]
    dev = jnp.stack([lax.axis_index("ctx").astype(i32), jnp.int32(tokens)])
    args = (dev, query_rows, key_rows, value_rows, out_gain, doc_starts)
    near, hops = core(False, *args)
    return lax.cond(hops[0] > 0, lambda near, *args: core(True, *args)[0], lambda near, *args: near, near, *args)


def solution(mesh):
    placed = (P("ctx", "head"), P("ctx", "head"), P("ctx", "head"), P("head"), P())
    return jax.shard_map(
        shards, mesh=mesh, in_specs=placed, out_specs=P("ctx", "head"), check_vma=False
    )
```
